768 devices in a mesh: dp: 8 (over x, core), row: 12 (over z), col: 8 (over y).
Axes of the slice: x: 4, y: 8, z: 12, core: 2. Of those that a mesh axis runs over, the one named last changes fastest.
Arguments:
- inputs: bfloat16 [2048, 9216], P('dp', 'row'), may hold values from -24 to 24
- out_grad: bfloat16 [2048, 49152], P('dp', 'col'), may hold values from -0.22097087 to 0.22097087
- weight: bfloat16 [49152, 9216], P(('col', 'dp'), 'row'), may hold values from -3 to 3
- ff_old: float32 [49152], P(('col', 'dp')), may hold values from 0.1 to 4
- d_old: float32 [9216], P('row'), may hold values from 0.05 to 0.5
Outputs:
- update: bfloat16 [49152, 9216], P(('col', 'dp'), 'row')
- new_weight: bfloat16 [49152, 9216], P(('col', 'dp'), 'row')
- ff_new: float32 [49152], P(('col', 'dp'))
- d_new: float32 [9216], P('row')
The draws below stay inside these ranges and needn't reach their ends.
All inputs are finite; a program needn't handle non-finite values.
Results may differ from the reference program's by a relative error of at most 0.018.
Values may be sent and summed in bfloat16 or wider, within the bound.
A program may use at most 64 MiB of HBM per device.

```python
import math
import jax
import jax.numpy as jnp
from jax import lax

D = 9216
FF = 49152
TOK_DEV = 256
TOKENS = 2048
N_DP = 8
N_ROW = 12
N_COL = 8


STRONG_LEAD = 1.6


STRONG_TRAIL = 1.0


WEAK_SIDE = 0.25


def token_group(key):
    return jax.random.randint(jax.random.fold_in(key, 101), (TOKENS,), 0, 2)


def side_strength(group, favored):
    leading = jnp.where(favored, STRONG_LEAD, WEAK_SIDE)
    trailing = jnp.where(favored, WEAK_SIDE, STRONG_TRAIL)
    return jnp.where(group[:, None] == 0, leading[None, :], trailing[None, :]).astype(jnp.float32)


def draw_inputs(key, part):
    group = token_group(key)
    key = jax.random.fold_in(key, 5)
    centre_key, noise_key, side_key = jax.random.split(key, 3)
    block_cols = D // N_ROW
    place = jnp.arange(D) // block_cols
    favored = (jax.random.permutation(side_key, N_ROW) < N_ROW // 2)[place]
    strength = side_strength(group, favored)
    common_scale = (TOKENS / 2.0) ** (-0.25)
    ramp = place.astype(jnp.float32) / float(max(N_ROW - 1, 1))
    amplitude = jnp.power(2.5, ramp)
    centre = jnp.clip(jax.random.normal(centre_key, (D,), jnp.float32), -2.5, 2.5)
    values = jnp.clip(jax.random.normal(noise_key, (TOKENS, D), jnp.float32), -4.0, 4.0)
    mixed = amplitude[None, :] * strength * (common_scale * centre[None, :] + values)
    return mixed.astype(jnp.bfloat16)


def draw_out_grad(key, part):
    group = token_group(key)
    key = jax.random.fold_in(key, 11)
    centre_key, noise_key, side_key = jax.random.split(key, 3)
    block_count = N_COL * N_DP
    place = jnp.arange(FF) // (FF // block_count)
    favored = (jax.random.permutation(side_key, block_count) < block_count // 2)[place]
    strength = side_strength(group, favored)
    common_scale = (TOKENS / 2.0) ** (-0.25)
    spread = TOKENS ** (-0.5)
    centre = jnp.clip(jax.random.normal(centre_key, (FF,), jnp.float32), -2.5, 2.5)
    values = jnp.clip(jax.random.normal(noise_key, (TOKENS, FF), jnp.float32), -4.0, 4.0)
    mixed = spread * strength * (common_scale * centre[None, :] + values)
    return mixed.astype(jnp.bfloat16)


def draw_ff_old(key, part):
    key = jax.random.fold_in(key, 23)
    block_rows = FF // (N_COL * N_DP)
    place = jnp.arange(FF) // block_rows % N_DP
    ramp = place.astype(jnp.float32) / float(max(N_DP - 1, 1))
    factor = jnp.exp(jax.random.uniform(key, (FF,), jnp.float32, -0.6931, 0.0))
    values = 3.0 * jnp.power(10.0, -ramp) * factor
    return values.astype(jnp.float32)


def levels(own_key, dims, cuts, low, largest):
    loudness, own = 1.0, jax.random.fold_in(own_key, 6)
    for position, blocks in cuts:
        heights = jnp.exp(jax.random.uniform(jax.random.fold_in(own, position), (blocks,), jnp.float32, low / len(cuts), largest / len(cuts)))
        loudness = loudness * jnp.repeat(heights, dims[position] // blocks).reshape([-1 if axis == position else 1 for axis in range(len(dims))])
    return loudness


def bell_draw(key, shape, deviation, most, shards=(), kind=jnp.bfloat16):
    values = jax.random.normal(key, shape, jnp.float32) * deviation
    if len(shards) > 0:
        values = levels(key, shape, shards, -0.22, 0.18) * values
    return jnp.clip(values, min=-most, max=most).astype(kind)


def setup_inputs(seed: int = 0) -> dict:
    keys = jax.random.split(jax.random.key(seed), 6)
    return {
        "inputs": draw_inputs(jax.random.fold_in(keys[5], 71), 0),
        "out_grad": draw_out_grad(jax.random.fold_in(keys[5], 71), 0),
        "weight": bell_draw(keys[2], (FF, D), 0.5, 3.0, ((0, 64), (1, 12))),
        "ff_old": draw_ff_old(jax.random.fold_in(keys[5], 71), 0),
        "d_old": jnp.clip(jnp.exp(math.log(0.5) - 2.3025851 * jax.random.uniform(keys[4], (D,), jnp.float32) ** levels(keys[4], (D,), ((0, 12),), -0.2, 0.2)), 0.05, 0.5),
    }


DECAY_RATE = 1.0 - 10.0 ** (-0.8)
SQUARE_EPS = 1e-30
LEARNING_RATE = 0.02

def reference(inputs, out_grad, weight, ff_old, d_old):
    blocked = math.gcd(FF, 512)
    amount = FF // blocked
    tokens_in = inputs.astype(jnp.float32).reshape(N_DP, TOK_DEV, D)
    segments = out_grad.reshape(TOKENS, amount, blocked).transpose(1, 0, 2)

    def block_gradient(segment):
        tokens_out = segment.astype(jnp.float32).reshape(N_DP, TOK_DEV, blocked)
        products = jnp.einsum('gtf,gtd->gfd', tokens_out, tokens_in, precision=lax.Precision.HIGHEST)
        rounded = lax.optimization_barrier(products.astype(jnp.bfloat16))
        return lax.optimization_barrier(jnp.sum(rounded.astype(jnp.float32), axis=0))
    gradient = lax.map(block_gradient, segments).reshape(FF, D)
    squares = gradient * gradient + SQUARE_EPS
    ff_new = DECAY_RATE * ff_old + (1.0 - DECAY_RATE) * lax.optimization_barrier(jnp.sum(squares, axis=1)) / D
    d_new = DECAY_RATE * d_old + (1.0 - DECAY_RATE) * lax.optimization_barrier(jnp.sum(squares, axis=0)) / FF
    ff_mean = jnp.sum(ff_new) / FF
    entries = float(FF * D)
    master = weight.astype(jnp.float32)
    scaled = gradient / jnp.sqrt(ff_new[:, None] * d_new[None, :] / ff_mean)
    clip_factor = jnp.maximum(1.0, jnp.sqrt(jnp.sum(scaled * scaled) / entries))
    clipped = scaled / clip_factor
    return (clipped.astype(jnp.bfloat16), (master - LEARNING_RATE * clipped).astype(jnp.bfloat16), ff_new, d_new)
```

```python
import functools

import jax
import jax.numpy as jnp
from jax import lax
from jax.experimental import pallas as pl
from jax.experimental.pallas import tpu as pltpu
from jax.sharding import PartitionSpec as P

D = 9216
FF = 49152

DECAY_RATE = 1.0 - 10.0 ** (-0.8)
SQUARE_EPS = 1e-30
LEARNING_RATE = 0.02

MESH = pl.DeviceIdType.MESH
LANES = 128


def kernel(sizes, d_full, ff_full, inp, og, w_hbm, ff_old, d_old, upd_ref, new_ref, ff_ref, d_ref,
           a_buf, b_buf, w_buf, g, row_t, ff_buf, xy_buf, col_buf, t_buf,
           a_send, a_recv, b_send, b_recv, loc, s_send, ff_recv, xy_recv, col_recv, t_recv):
    n_dp, n_row, n_col = sizes
    dp, row, col = (lax.axis_index(a) for a in ("dp", "row", "col"))
    tok, width = inp.shape
    units = g.shape[0]
    blocks = units // LANES
    lane_blocks = width // LANES

    barrier = pltpu.get_barrier_semaphore()
    for axis, n, me in (("dp", n_dp, dp), ("row", n_row, row), ("col", n_col, col)):
        def greet(i, _, axis=axis, n=n, me=me):
            pl.semaphore_signal(barrier, inc=1, device_id={axis: lax.rem(me + i, n)}, device_id_type=MESH)
            return 0
        lax.fori_loop(1, n, greet, 0)

    def unit_cols(i):
        return pl.ds(pl.multiple_of(i * units, LANES), units)

    own_a = pltpu.make_async_copy(og.at[:, unit_cols(dp)], a_buf.at[dp], loc.at[0])
    own_b = pltpu.make_async_copy(inp, b_buf.at[dp], loc.at[1])
    own_w = pltpu.make_async_copy(w_hbm, w_buf, loc.at[2])
    own_a.start()
    own_b.start()
    own_w.start()
    pl.semaphore_wait(barrier, n_dp + n_row + n_col - 3)

    def send_a(i):
        to = lax.rem(dp + i, n_dp)
        return pltpu.make_async_remote_copy(og.at[:, unit_cols(to)], a_buf.at[dp], a_send.at[i], a_recv.at[dp],
                                            device_id={"dp": to}, device_id_type=MESH)

    def send_b(i):
        to = lax.rem(dp + i, n_dp)
        return pltpu.make_async_remote_copy(inp, b_buf.at[dp], b_send.at[i], b_recv.at[dp],
                                            device_id={"dp": to}, device_id_type=MESH)

    def start_sends(i, _):
        send_a(i).start()
        send_b(i).start()
        return 0
    lax.fori_loop(1, n_dp, start_sends, 0)

    def product(src):
        return lax.dot_general(a_buf[src], b_buf[src], (((0,), (0,)), ((), ())), preferred_element_type=jnp.float32)

    own_a.wait()
    own_b.wait()
    g[...] = product(dp)

    def take(i, _):
        src = lax.rem(dp + n_dp - i, n_dp)
        pltpu.make_async_remote_copy(a_buf.at[src], a_buf.at[src], a_send.at[0], a_recv.at[src],
                                     device_id={"dp": src}, device_id_type=MESH).wait_recv()
        pltpu.make_async_remote_copy(b_buf.at[src], b_buf.at[src], b_send.at[0], b_recv.at[src],
                                     device_id={"dp": src}, device_id_type=MESH).wait_recv()
        g[...] += product(src)
        return 0
    lax.fori_loop(1, n_dp, take, 0)

    def exchange(axis, n, me, buf, recv):
        def copy(i):
            to = lax.rem(me + i, n)
            return pltpu.make_async_remote_copy(buf.at[me], buf.at[me], s_send.at[i], recv.at[me],
                                                device_id={axis: to}, device_id_type=MESH)

        def start(i, _):
            copy(i).start()
            return 0
        lax.fori_loop(1, n, start, 0)

        def arrive(i, _):
            src = lax.rem(me + n - i, n)
            pltpu.make_async_remote_copy(buf.at[src], buf.at[src], s_send.at[0], recv.at[src],
                                         device_id={axis: src}, device_id_type=MESH).wait_recv()
            return 0
        lax.fori_loop(1, n, arrive, 0)

        def sent(i, _):
            copy(i).wait_send()
            return 0
        lax.fori_loop(1, n, sent, 0)
        total = buf[0]
        for i in range(1, n):
            total = total + buf[i]
        return total

    ff_buf[row] = jnp.zeros(ff_buf.shape[1:], jnp.float32)
    xy_buf[dp] = jnp.zeros(xy_buf.shape[1:], jnp.float32)
    d_part = [jnp.zeros((1, LANES), jnp.float32)] * lane_blocks
    for k in range(blocks):
        rows = pl.ds(k * LANES, LANES)
        part = None
        for j in range(lane_blocks):
            v = g[rows, pl.ds(j * LANES, LANES)]
            sq = v * v + SQUARE_EPS
            part = sq if part is None else part + sq
            d_part[j] = d_part[j] + jnp.sum(sq, axis=0, keepdims=True)
        ff_buf[row, pl.ds(k, 1), :] = jnp.sum(part.T, axis=0, keepdims=True)
    for j in range(lane_blocks):
        xy_buf[dp, pl.ds(j, 1), :] = d_part[j]

    ff_total = exchange("row", n_row, row, ff_buf, ff_recv)[:blocks]
    ff_new = DECAY_RATE * ff_old[...] + (1.0 - DECAY_RATE) * ff_total / d_full
    ff_ref[...] = ff_new
    inv = 1.0 / ff_new

    q_part = [jnp.zeros((1, LANES), jnp.float32)] * lane_blocks
    for k in range(blocks):
        rows = pl.ds(k * LANES, LANES)
        u = jnp.broadcast_to(inv[k:k + 1], (LANES, LANES)).T
        for j in range(lane_blocks):
            v = g[rows, pl.ds(j * LANES, LANES)]
            q_part[j] = q_part[j] + jnp.sum(v * v * u, axis=0, keepdims=True)
    for j in range(lane_blocks):
        xy_buf[dp, pl.ds(lane_blocks + j, 1), :] = q_part[j]
    xy_buf[dp, pl.ds(2 * lane_blocks, 1), :] = jnp.sum(ff_new, axis=0, keepdims=True)

    col_buf[col] = exchange("dp", n_dp, dp, xy_buf, xy_recv)
    total = exchange("col", n_col, col, col_buf, col_recv)
    d_new = DECAY_RATE * d_old[...] + (1.0 - DECAY_RATE) * total[:lane_blocks] / ff_full
    d_ref[...] = d_new
    ff_mean = jnp.sum(total[2 * lane_blocks:2 * lane_blocks + 1], axis=1, keepdims=True) / ff_full
    t_buf[row] = jnp.zeros(t_buf.shape[1:], jnp.float32)
    t_buf[row, pl.ds(0, lane_blocks), :] = total[lane_blocks:2 * lane_blocks] / d_new
    t_total = exchange("row", n_row, row, t_buf, t_recv)
    square_mean = jnp.sum(jnp.sum(t_total, axis=0, keepdims=True), axis=1, keepdims=True) * ff_mean / (d_full * ff_full)
    factor = jnp.sqrt(ff_mean) / jnp.maximum(1.0, jnp.sqrt(square_mean))
    own_w.wait()
    inv_d = lax.rsqrt(d_new) * factor
    inv_f = lax.rsqrt(ff_new)
    for k in range(blocks):
        rows = pl.ds(k * LANES, LANES)
        u = jnp.broadcast_to(inv_f[k:k + 1], (LANES, LANES)).T
        for j in range(lane_blocks):
            cols = pl.ds(j * LANES, LANES)
            clipped = g[rows, cols] * u * inv_d[j:j + 1]
            upd_ref[rows, cols] = clipped.astype(jnp.bfloat16)
            new_ref[rows, cols] = (w_buf[rows, cols].astype(jnp.float32) - LEARNING_RATE * clipped).astype(jnp.bfloat16)

    def drain(i, _):
        send_a(i).wait_send()
        send_b(i).wait_send()
        return 0
    lax.fori_loop(1, n_dp, drain, 0)


def solution(mesh):
    sizes = n_dp, n_row, n_col = tuple(mesh.shape[a] for a in ("dp", "row", "col"))

    def body(inputs, out_grad, weight, ff_old, d_old):
        tok, width = inputs.shape
        units = weight.shape[0]
        hbm = pl.BlockSpec(memory_space=pl.ANY)
        vmem = pl.BlockSpec(memory_space=pltpu.VMEM)
        f32, bf16 = jnp.float32, jnp.bfloat16
        fr, dr = units // LANES, width // LANES
        dma = pltpu.SemaphoreType.DMA
        upd, new, ff_new, d_new = pl.pallas_call(
            functools.partial(kernel, sizes, float(width * n_row), float(units * n_dp * n_col)),
            out_shape=(
                jax.ShapeDtypeStruct((units, width), bf16),
                jax.ShapeDtypeStruct((units, width), bf16),
                jax.ShapeDtypeStruct((fr, LANES), f32),
                jax.ShapeDtypeStruct((dr, LANES), f32),
            ),
            in_specs=[hbm, hbm, hbm, vmem, vmem],
            out_specs=(vmem, vmem, vmem, vmem),
            scratch_shapes=[
                pltpu.VMEM((n_dp, tok, units), bf16),
                pltpu.VMEM((n_dp, tok, width), bf16),
                pltpu.VMEM((units, width), bf16),
                pltpu.VMEM((units, width), f32),
                pltpu.VMEM((units, LANES), f32),
                pltpu.VMEM((n_row, 8, LANES), f32),
                pltpu.VMEM((n_dp, 16, LANES), f32),
                pltpu.VMEM((n_col, 16, LANES), f32),
                pltpu.VMEM((n_row, 8, LANES), f32),
                dma((n_dp,)), dma((n_dp,)), dma((n_dp,)), dma((n_dp,)), dma((3,)),
                dma((max(sizes),)), dma((n_row,)), dma((n_dp,)), dma((n_col,)), dma((n_row,)),
            ],
            compiler_params=pltpu.CompilerParams(collective_id=0, has_side_effects=True, vmem_limit_bytes=50 * 2**20),
        )(inputs, out_grad, weight, ff_old.reshape(fr, LANES), d_old.reshape(dr, LANES))
        return upd, new, ff_new.reshape(units), d_new.reshape(width)

    return jax.shard_map(
        body,
        mesh=mesh,
        in_specs=(
            P("dp", "row"),
            P("dp", "col"),
            P(("col", "dp"), "row"),
            P(("col", "dp")),
            P("row"),
        ),
        out_specs=(P(("col", "dp"), "row"), P(("col", "dp"), "row"), P(("col", "dp")), P("row")),
        check_vma=False,
    )
```

```python
import functools

import jax
import jax.numpy as jnp
from jax import lax
from jax.experimental import pallas as pl
from jax.experimental.pallas import tpu as pltpu
from jax.sharding import PartitionSpec as P

D = 9216
FF = 49152

DECAY_RATE = 1.0 - 10.0 ** (-0.8)
SQUARE_EPS = 1e-30
LEARNING_RATE = 0.02

MESH = pl.DeviceIdType.MESH
LANES = 128
PIECES = 3
QUARTERS = 4


def gather_kernel(sizes, d_full, ff_full, inp, og, ff_old, d_old, g_ref, ff_ref, d_ref, fac_ref,
                  a_buf, b_buf, ff_prev, d_prev, ff_buf, xy_buf, col_buf, t_buf,
                  a_send, a_recv, z_send, b_send, b_recv, y_send, c_send, c_recv, loc,
                  s_send, ff_recv, xy_recv, col_recv, t_recv):
    n_dp, n_row, n_col = sizes
    n_x = n_dp // 2
    dp, row, col = (lax.axis_index(a) for a in ("dp", "row", "col"))
    x = dp // 2
    core = dp - 2 * x
    sib = 2 * x + 1 - core
    m = lax.rem(row, PIECES)
    q = lax.rem(col, QUARTERS)
    tok, width = inp.shape
    units = g_ref.shape[0]
    piece = units // PIECES
    quarter = tok // QUARTERS
    half = quarter // 2
    blocks = units // LANES
    lane_blocks = width // LANES

    barrier = pltpu.get_barrier_semaphore()
    for axis, n, me in (("dp", n_dp, dp), ("row", n_row, row), ("col", n_col, col)):
        def greet(i, _, axis=axis, n=n, me=me):
            pl.semaphore_signal(barrier, inc=1, device_id={axis: lax.rem(me + i, n)}, device_id_type=MESH)
            return 0
        lax.fori_loop(1, n, greet, 0)

    def og_piece(to, p):
        return og.at[:, pl.ds(pl.multiple_of(to * units + p * piece, LANES), piece)]

    def rows_of(start, size):
        return pl.ds(pl.multiple_of(start, 16), size)

    own = [pltpu.make_async_copy(og_piece(dp, p), a_buf.at[p, dp], loc.at[p]) for p in range(PIECES)]
    own.append(pltpu.make_async_copy(inp, b_buf.at[dp], loc.at[3]))
    own.append(pltpu.make_async_copy(ff_old, ff_prev, loc.at[4]))
    own.append(pltpu.make_async_copy(d_old, d_prev, loc.at[5]))
    for c in own:
        c.start()

    def far(dx, flip):
        there = lax.rem(x + dx + n_x, n_x)
        return 2 * there + (1 - core if flip else core)

    def send_a(k, dx, flip):
        to = far(dx, flip)
        return pltpu.make_async_remote_copy(og_piece(to, m), a_buf.at[m, dp], a_send.at[k], a_recv.at[0, dp],
                                            device_id={"dp": to}, device_id_type=MESH)

    def send_sib_a(j):
        p = lax.rem(m + j, PIECES)
        return pltpu.make_async_remote_copy(og_piece(sib, p), a_buf.at[p, dp], c_send.at[j], a_recv.at[j, dp],
                                            device_id={"dp": sib}, device_id_type=MESH)

    def send_sib_b(k, src):
        return pltpu.make_async_remote_copy(b_buf.at[src], b_buf.at[src], c_send.at[PIECES + k], c_recv.at[src],
                                            device_id={"dp": sib}, device_id_type=MESH)

    def send_b(k, dx):
        part = rows_of(q * quarter, quarter)
        return pltpu.make_async_remote_copy(inp.at[part], b_buf.at[dp, part], b_send.at[k], b_recv.at[0, dp],
                                            device_id={"dp": far(dx, False)}, device_id_type=MESH)

    def pass_z(src, j):
        to = lax.rem(row + (n_row - 1 if j == 1 else 1), n_row)
        return pltpu.make_async_remote_copy(a_buf.at[m, src], a_buf.at[m, src], z_send.at[j - 1, src], a_recv.at[j, src],
                                            device_id={"row": to}, device_id_type=MESH)

    def pass_y(src, j):
        step = (1, -1, 2, -2)[j - 1]
        start, size = q * quarter, quarter
        if j >= 3:
            start, size = start + (j - 3) * half, half
        part = rows_of(start, size)
        return pltpu.make_async_remote_copy(b_buf.at[src, part], b_buf.at[src, part], y_send.at[j - 1, src], b_recv.at[j, src],
                                            device_id={"col": lax.rem(col + step + n_col, n_col)}, device_id_type=MESH)

    def got_a(j, src):
        p = lax.rem(m + j, PIECES)
        pltpu.make_async_remote_copy(a_buf.at[p, src], a_buf.at[p, src], a_send.at[0], a_recv.at[j, src],
                                     device_id={"dp": sib}, device_id_type=MESH).wait_recv()

    def got_b(j, src):
        shift = (0, -1, 1, -2, 2)[j]
        start, size = lax.rem(q + shift + QUARTERS, QUARTERS) * quarter, quarter
        if j >= 3:
            start, size = start + (j - 3) * half, half
        part = rows_of(start, size)
        pltpu.make_async_remote_copy(b_buf.at[src, part], b_buf.at[src, part], b_send.at[0], b_recv.at[j, src],
                                     device_id={"dp": sib}, device_id_type=MESH).wait_recv()

    def got_c(src):
        pltpu.make_async_remote_copy(b_buf.at[src], b_buf.at[src], b_send.at[0], c_recv.at[src],
                                     device_id={"dp": sib}, device_id_type=MESH).wait_recv()

    near = ((1, False), (-1, False), (1, True), (-1, True))
    away = ((2, False), (2, True))
    steps = (1, -1, 2)
    sends = [send_a(k, *t) for k, t in enumerate(near)]
    sends += [send_b(k, dx) for k, dx in enumerate(steps)]
    sends += [send_a(len(near) + k, *t) for k, t in enumerate(away)]
    sends += [send_sib_a(j) for j in range(PIECES)]

    pl.semaphore_wait(barrier, n_dp + n_row + n_col - 3)
    for c in sends:
        c.start()
    own[3].wait()
    c = send_sib_b(0, dp)
    c.start()
    sends.append(c)

    def product(j, src, first=False):
        p = lax.rem(m + j, PIECES)
        out = g_ref.at[pl.ds(pl.multiple_of(p * piece, LANES), piece)]
        value = lax.dot_general(a_buf[p, src], b_buf[src], (((0,), (0,)), ((), ())), preferred_element_type=jnp.float32)
        out[...] = value if first else out[...] + value

    for c in own[:3]:
        c.wait()
    for j in range(PIECES):
        product(j, dp, first=True)

    def relay_a(dx, flip):
        src = far(dx, flip)
        got_a(0, src)
        for j in (1, 2):
            c = pass_z(src, j)
            c.start()
            sends.append(c)

    for t in near:
        relay_a(*t)
    for dx in steps:
        src = far(dx, False)
        got_b(0, src)
        for j in (1, 2, 3, 4):
            c = pass_y(src, j)
            c.start()
            sends.append(c)
    got_c(sib)
    for j in range(PIECES):
        got_a(j, sib)
        product(j, sib)
    for t in away:
        relay_a(*t)
    for k, dx in enumerate(steps):
        src = far(dx, False)
        for j in (1, 2, 3, 4):
            got_b(j, src)
        c = send_sib_b(1 + k, src)
        c.start()
        sends.append(c)
        product(0, src)
    for dx in steps:
        src = far(dx, True)
        got_c(src)
        product(0, src)
    for t in near + away:
        src = far(*t)
        for j in (1, 2):
            got_a(j, src)
            product(j, src)

    def exchange(axis, n, me, buf, recv, meanwhile=None):
        def copy(i):
            to = lax.rem(me + i, n)
            return pltpu.make_async_remote_copy(buf.at[me], buf.at[me], s_send.at[i], recv.at[me],
                                                device_id={axis: to}, device_id_type=MESH)

        def start(i, _):
            copy(i).start()
            return 0
        lax.fori_loop(1, n, start, 0)
        if meanwhile is not None:
            meanwhile()

        def arrive(i, _):
            src = lax.rem(me + n - i, n)
            pltpu.make_async_remote_copy(buf.at[src], buf.at[src], s_send.at[0], recv.at[src],
                                         device_id={axis: src}, device_id_type=MESH).wait_recv()
            return 0
        lax.fori_loop(1, n, arrive, 0)

        def sent(i, _):
            copy(i).wait_send()
            return 0
        lax.fori_loop(1, n, sent, 0)
        total = buf[0]
        for i in range(1, n):
            total = total + buf[i]
        return total

    ff_buf[row] = jnp.zeros(ff_buf.shape[1:], jnp.float32)
    xy_buf[dp] = jnp.zeros(xy_buf.shape[1:], jnp.float32)
    d_part = [jnp.zeros((1, LANES), jnp.float32)] * lane_blocks
    for k in range(blocks):
        rows = pl.ds(k * LANES, LANES)
        part = None
        for j in range(lane_blocks):
            v = g_ref[rows, pl.ds(j * LANES, LANES)]
            sq = v * v + SQUARE_EPS
            part = sq if part is None else part + sq
            d_part[j] = d_part[j] + jnp.sum(sq, axis=0, keepdims=True)
        ff_buf[row, pl.ds(k, 1), :] = jnp.sum(part.T, axis=0, keepdims=True)
    for j in range(lane_blocks):
        xy_buf[dp, pl.ds(j, 1), :] = d_part[j]

    own[4].wait()
    own[5].wait()
    ff_total = exchange("row", n_row, row, ff_buf, ff_recv)[:blocks]
    ff_new = DECAY_RATE * ff_prev[...] + (1.0 - DECAY_RATE) * ff_total / d_full
    ff_ref[...] = ff_new
    inv = 1.0 / ff_new

    q_part = [jnp.zeros((1, LANES), jnp.float32)] * lane_blocks
    for k in range(blocks):
        rows = pl.ds(k * LANES, LANES)
        u = jnp.broadcast_to(inv[k:k + 1], (LANES, LANES)).T
        for j in range(lane_blocks):
            v = g_ref[rows, pl.ds(j * LANES, LANES)]
            q_part[j] = q_part[j] + jnp.sum(v * v * u, axis=0, keepdims=True)
    for j in range(lane_blocks):
        xy_buf[dp, pl.ds(lane_blocks + j, 1), :] = q_part[j]
    xy_buf[dp, pl.ds(2 * lane_blocks, 1), :] = jnp.sum(ff_new, axis=0, keepdims=True)

    col_buf[col] = exchange("dp", n_dp, dp, xy_buf, xy_recv)
    total = exchange("col", n_col, col, col_buf, col_recv)
    d_new = DECAY_RATE * d_prev[...] + (1.0 - DECAY_RATE) * total[:lane_blocks] / ff_full
    d_ref[...] = d_new
    ff_mean = jnp.sum(total[2 * lane_blocks:2 * lane_blocks + 1], axis=1, keepdims=True) / ff_full
    t_buf[row] = jnp.zeros(t_buf.shape[1:], jnp.float32)
    t_buf[row, pl.ds(0, lane_blocks), :] = total[lane_blocks:2 * lane_blocks] / d_new
    inv_d = lax.rsqrt(d_new)
    inv_f = lax.rsqrt(ff_new)

    def scale():
        for k in range(blocks):
            rows = pl.ds(k * LANES, LANES)
            u = jnp.broadcast_to(inv_f[k:k + 1], (LANES, LANES)).T
            for j in range(lane_blocks):
                cols = pl.ds(j * LANES, LANES)
                g_ref[rows, cols] = g_ref[rows, cols] * u * inv_d[j:j + 1]

    t_total = exchange("row", n_row, row, t_buf, t_recv, scale)
    square_mean = jnp.sum(jnp.sum(t_total, axis=0, keepdims=True), axis=1, keepdims=True) * ff_mean / (d_full * ff_full)
    factor = jnp.sqrt(ff_mean) / jnp.maximum(1.0, jnp.sqrt(square_mean))
    fac_ref[...] = jnp.broadcast_to(factor, fac_ref.shape)
    for c in sends:
        c.wait_send()


def write_kernel(g, fac, w, ff_in, d_in, upd, new, ff_out, d_out, upd_buf, new_buf, sem):
    copies = [pltpu.make_async_copy(ff_in, ff_out, sem.at[0, 0]), pltpu.make_async_copy(d_in, d_out, sem.at[1, 0])]
    for c in copies:
        c.start()
    factor = fac[0:1, 0:1]
    for k in range(g.shape[0] // LANES):
        rows = pl.ds(k * LANES, LANES)
        clipped = g[rows, :] * factor
        upd_buf[rows, :] = clipped.astype(jnp.bfloat16)
        new_buf[rows, :] = (w[rows, :].astype(jnp.float32) - LEARNING_RATE * clipped).astype(jnp.bfloat16)
        for i, (src, dst) in enumerate(((upd_buf, upd), (new_buf, new))):
            c = pltpu.make_async_copy(src.at[rows], dst.at[rows], sem.at[i, k + 1])
            c.start()
            copies.append(c)
    for c in copies:
        c.wait()


def solution(mesh):
    sizes = n_dp, n_row, n_col = tuple(mesh.shape[a] for a in ("dp", "row", "col"))

    def body(inputs, out_grad, weight, ff_old, d_old):
        tok, width = inputs.shape
        units = weight.shape[0]
        hbm = pl.BlockSpec(memory_space=pltpu.HBM)
        vmem = pl.BlockSpec(memory_space=pltpu.VMEM)
        f32, bf16 = jnp.float32, jnp.bfloat16
        fr, dr = units // LANES, width // LANES
        dma = pltpu.SemaphoreType.DMA
        shape = jax.ShapeDtypeStruct
        g, ff_new, d_new, fac = pl.pallas_call(
            functools.partial(gather_kernel, sizes, float(width * n_row), float(units * n_dp * n_col)),
            out_shape=(shape((units, width), f32), shape((fr, LANES), f32), shape((dr, LANES), f32), shape((8, LANES), f32)),
            in_specs=[hbm] * 4,
            out_specs=(vmem,) * 4,
            scratch_shapes=[
                pltpu.VMEM((PIECES, n_dp, tok, units // PIECES), bf16),
                pltpu.VMEM((n_dp, tok, width), bf16),
                pltpu.VMEM((fr, LANES), f32),
                pltpu.VMEM((dr, LANES), f32),
                pltpu.VMEM((n_row, 8, LANES), f32),
                pltpu.VMEM((n_dp, 16, LANES), f32),
                pltpu.VMEM((n_col, 16, LANES), f32),
                pltpu.VMEM((n_row, 8, LANES), f32),
                dma((6,)), dma((PIECES, n_dp)), dma((2, n_dp)),
                dma((3,)), dma((5, n_dp)), dma((4, n_dp)),
                dma((PIECES + 4,)), dma((n_dp,)), dma((6,)),
                dma((max(sizes),)), dma((n_row,)), dma((n_dp,)), dma((n_col,)), dma((n_row,)),
            ],
            compiler_params=pltpu.CompilerParams(collective_id=0, has_side_effects=True, vmem_limit_bytes=51 * 2**20),
            name="gather_product_stats",
        )(inputs, out_grad, ff_old.reshape(fr, LANES), d_old.reshape(dr, LANES))
        upd, new, ff_out, d_out = pl.pallas_call(
            write_kernel,
            out_shape=(shape((units, width), bf16), shape((units, width), bf16), shape((fr, LANES), f32), shape((dr, LANES), f32)),
            in_specs=[vmem] * 5,
            out_specs=(hbm,) * 4,
            scratch_shapes=[
                pltpu.VMEM((units, width), bf16),
                pltpu.VMEM((units, width), bf16),
                dma((2, fr + 1)),
            ],
            compiler_params=pltpu.CompilerParams(vmem_limit_bytes=40 * 2**20),
            name="write_results",
        )(g, fac, weight, ff_new, d_new)
        return upd, new, ff_out.reshape(units), d_out.reshape(width)

    return jax.shard_map(
        body,
        mesh=mesh,
        in_specs=(
            P("dp", "row"),
            P("dp", "col"),
            P(("col", "dp"), "row"),
            P(("col", "dp")),
            P("row"),
        ),
        out_specs=(P(("col", "dp"), "row"), P(("col", "dp"), "row"), P(("col", "dp")), P("row")),
        check_vma=False,
    )
```

```python
import functools

import jax
import jax.numpy as jnp
from jax import lax
from jax.experimental import pallas as pl
from jax.experimental.pallas import tpu as pltpu
from jax.sharding import PartitionSpec as P

D = 9216
FF = 49152

DECAY_RATE = 1.0 - 10.0 ** (-0.8)
SQUARE_EPS = 1e-30
LEARNING_RATE = 0.02

MESH = pl.DeviceIdType.MESH
LANES = 128
PIECES = 3
QUARTERS = 4


def gather_kernel(sizes, d_full, ff_full, inp, og, ff_old, d_old, g_out, ff_out, d_out, fac_out,
                  g_ref, a_buf, b_buf, ff_prev, d_prev, ff_res, d_res, fac_res, ff_buf, d_buf, dcol_buf, q_buf, xy_buf, t_buf,
                  a_send, a_recv, z_send, b_send, b_recv, y_send, c_send, sib_send, c_recv, loc, out_sem,
                  ff_sems, d_sems, dcol_sems, xy_sems, t_sems, heard):
    n_dp, n_row, n_col = sizes
    n_x = n_dp // 2
    dp, row, col = (lax.axis_index(a) for a in ("dp", "row", "col"))
    x = dp // 2
    core = dp - 2 * x
    sib = 2 * x + 1 - core
    m = lax.rem(row, PIECES)
    q = lax.rem(col, QUARTERS)
    tok, width = inp.shape
    units = g_ref.shape[0]
    piece = units // PIECES
    quarter = tok // QUARTERS
    half = quarter // 2
    blocks = units // LANES
    lane_blocks = width // LANES

    barrier = pltpu.get_barrier_semaphore()
    def others(axis, n, me):
        order = sorted(range(1, n), key=lambda t: -min(t, n - t))
        return [{axis: lax.rem(me + t, n)} for t in order]

    rows_far, cols_far, dps_far = others("row", n_row, row), others("col", n_col, col), others("dp", n_dp, dp)
    greeted = rows_far[-2:] + cols_far[-4:] + dps_far
    for there in greeted:
        pl.semaphore_signal(barrier, inc=1, device_id=there, device_id_type=MESH)

    def og_piece(to, p):
        return og.at[:, pl.ds(pl.multiple_of(to * units + p * piece, LANES), piece)]

    def rows_of(start, size):
        return pl.ds(pl.multiple_of(start, 16), size)

    own = [pltpu.make_async_copy(og_piece(dp, p), a_buf.at[p, dp], loc.at[p]) for p in range(PIECES)]
    own.append(pltpu.make_async_copy(inp, b_buf.at[dp], loc.at[3]))
    own.append(pltpu.make_async_copy(ff_old, ff_prev, loc.at[4]))
    own.append(pltpu.make_async_copy(d_old, d_prev, loc.at[5]))
    for c in own:
        c.start()

    def far(dx, flip):
        there = lax.rem(x + dx + n_x, n_x)
        return 2 * there + (1 - core if flip else core)

    def send_a(k, dx, flip):
        to = far(dx, flip)
        return pltpu.make_async_remote_copy(og_piece(to, m), a_buf.at[m, dp], a_send.at[k], a_recv.at[0, dp],
                                            device_id={"dp": to}, device_id_type=MESH)

    def send_sib_a(j):
        p = lax.rem(m + j, PIECES)
        return pltpu.make_async_remote_copy(og_piece(sib, p), a_buf.at[p, dp], sib_send.at[j], a_recv.at[j, dp],
                                            device_id={"dp": sib}, device_id_type=MESH)

    def send_b(k, dx):
        part = rows_of(q * quarter, quarter)
        return pltpu.make_async_remote_copy(inp.at[part], b_buf.at[dp, part], b_send.at[k], b_recv.at[0, dp],
                                            device_id={"dp": far(dx, False)}, device_id_type=MESH)

    def pass_z(src, j):
        to = lax.rem(row + (n_row - 1 if j == 1 else 1), n_row)
        return pltpu.make_async_remote_copy(a_buf.at[m, src], a_buf.at[m, src], z_send.at[j - 1, src], a_recv.at[j, src],
                                            device_id={"row": to}, device_id_type=MESH)

    def pass_y(src, j):
        step = (1, -1, 2, -2)[j - 1]
        start, size = q * quarter, quarter
        if j >= 3:
            start, size = start + (j - 3) * half, half
        part = rows_of(start, size)
        return pltpu.make_async_remote_copy(b_buf.at[src, part], b_buf.at[src, part], y_send.at[j - 1, src], b_recv.at[j, src],
                                            device_id={"col": lax.rem(col + step + n_col, n_col)}, device_id_type=MESH)

    def part_of(j):
        shift = (0, -1, 1, -2, 2)[j]
        start, size = lax.rem(q + shift + QUARTERS, QUARTERS) * quarter, quarter
        if j >= 3:
            start, size = start + (j - 3) * half, half
        return rows_of(start, size)

    def share(src, j):
        part = part_of(j)
        return pltpu.make_async_remote_copy(b_buf.at[src, part], b_buf.at[src, part], c_send.at[j, src], c_recv.at[j, src],
                                            device_id={"dp": sib}, device_id_type=MESH)

    def got_a(j, src):
        p = lax.rem(m + j, PIECES)
        pltpu.make_async_remote_copy(a_buf.at[p, src], a_buf.at[p, src], a_send.at[0], a_recv.at[j, src],
                                     device_id={"dp": sib}, device_id_type=MESH).wait_recv()

    def got_b(j, src, recv):
        part = part_of(j)
        pltpu.make_async_remote_copy(b_buf.at[src, part], b_buf.at[src, part], b_send.at[0], recv.at[j, src],
                                     device_id={"dp": sib}, device_id_type=MESH).wait_recv()

    near = ((1, False), (-1, False), (1, True), (-1, True))
    away = ((2, False), (2, True))
    steps = (1, -1, 2)
    order = ("n0", "n1", "b0", "b1", "n2", "n3", "w0", "b2", "w1")
    moves = {}
    for k, t in enumerate(near):
        moves["n" + str(k)] = send_a(k, *t)
    for k, t in enumerate(away):
        moves["w" + str(k)] = send_a(len(near) + k, *t)
    for k, dx in enumerate(steps):
        moves["b" + str(k)] = send_b(k, dx)
    sends = [moves[k] for k in order]
    sends += [send_sib_a(j) for j in range(PIECES)]

    pl.semaphore_wait(barrier, len(greeted))

    def hail():
        for i, there in enumerate(rows_far[-2:]):
            pl.semaphore_signal(heard.at[i], inc=1, device_id=there, device_id_type=MESH)

    def answered():
        for i in range(2):
            pl.semaphore_wait(heard.at[i], 1)

    hail()
    for c in sends:
        c.start()

    def go(c):
        c.start()
        sends.append(c)

    own[3].wait()
    go(pltpu.make_async_remote_copy(b_buf.at[dp], b_buf.at[dp], sib_send.at[PIECES], c_recv.at[0, dp],
                                    device_id={"dp": sib}, device_id_type=MESH))

    def product(j, chip, first=False):
        p = lax.rem(m + j, PIECES)
        out = g_ref.at[pl.ds(pl.multiple_of(p * piece, LANES), piece)]
        pair = pl.ds(2 * chip, 2)
        value = lax.dot_general(a_buf[p, pair].reshape(2 * tok, piece), b_buf[pair].reshape(2 * tok, width),
                                (((0,), (0,)), ((), ())), preferred_element_type=jnp.float32)
        out[...] = value if first else out[...] + value

    def relay_a(dx, flip):
        src = far(dx, flip)
        got_a(0, src)
        go(pass_z(src, 1))
        go(pass_z(src, 2))

    def relay_b(dx):
        src = far(dx, False)
        got_b(0, src, b_recv)
        for j in (1, 2, 3, 4):
            go(pass_y(src, j))
        go(share(src, 0))

    def collect_b(dx):
        src = far(dx, False)
        for j in (1, 2, 3, 4):
            got_b(j, src, b_recv)
            go(share(src, j))

    def take(dx, j):
        got_a(j, far(dx, False)) if j else None
        got_a(j, far(dx, True)) if j else None
        product(j, lax.rem(x + dx + n_x, n_x))

    def relay(name):
        k = int(name[1])
        if name[0] == "b":
            relay_b(steps[k])
        else:
            relay_a(*(near if name[0] == "n" else away)[k])

    for k, name in enumerate(order[:-2]):
        relay(name)
        if k in (1, 4, 6):
            answered()
            hail()
    for c in own[:3]:
        c.wait()
    pltpu.make_async_remote_copy(b_buf.at[sib], b_buf.at[sib], b_send.at[0], c_recv.at[0, sib],
                                 device_id={"dp": sib}, device_id_type=MESH).wait_recv()
    for j in range(PIECES):
        got_a(j, sib)
        product(j, x, first=True)
    collect_b(steps[0])
    relay(order[-2])
    collect_b(steps[1])
    answered()
    hail()
    relay(order[-1])
    collect_b(steps[2])
    answered()
    own[4].wait()
    own[5].wait()

    d_part = [jnp.zeros((8, LANES), jnp.float32)] * lane_blocks

    def squares(j):
        p = lax.rem(m + j, PIECES)
        for i in range(piece // LANES):
            rows = pl.ds(pl.multiple_of(p * piece, LANES) + i * LANES, LANES)
            part = None
            for k in range(lane_blocks):
                v = g_ref[rows, pl.ds(k * LANES, LANES)]
                sq = v * v + SQUARE_EPS
                part = sq if part is None else part + sq
                d_part[k] = d_part[k] + jnp.sum(sq.reshape(LANES // 8, 8, LANES), axis=0)
            ff_buf[row, pl.ds(p * (piece // LANES) + i, 1), :] = jnp.sum(part.T, axis=0, keepdims=True)

    for dx in steps:
        for j in range(5):
            got_b(j, far(dx, True), c_recv)
        for j in range(PIECES):
            take(dx, j)
            if dx == steps[-1]:
                squares(j)
    for k in range(lane_blocks):
        d_buf[dp, pl.ds(k, 1), :] = jnp.sum(d_part[k], axis=0, keepdims=True)

    def spread(buf, me, sems, targets):
        for there in targets:
            pltpu.make_async_remote_copy(buf.at[me], buf.at[me], sems.at[0], sems.at[1],
                                         device_id=there, device_id_type=MESH).start()

    def slots(buf, sems):
        rest = buf.at[pl.ds(0, buf.shape[0] - 1)]
        return pltpu.make_async_remote_copy(rest, rest, sems.at[0], sems.at[1], device_id={"dp": sib}, device_id_type=MESH)

    def collect(buf, sems):
        slots(buf, sems).wait_recv()
        terms = [buf[k] for k in range(buf.shape[0])]
        while len(terms) > 1:
            terms = [sum(terms[k + 1:k + 2], terms[k]) for k in range(0, len(terms), 2)]
        return terms[0]

    outs = []

    def put(src, dst, k):
        c = pltpu.make_async_copy(src, dst, out_sem.at[k])
        c.start()
        outs.append(c)

    spread(d_buf, dp, d_sems, dps_far)
    spread(ff_buf, row, ff_sems, rows_far)
    dcol_buf[col] = collect(d_buf, d_sems)
    spread(dcol_buf, col, dcol_sems, cols_far)
    ff_new = DECAY_RATE * ff_prev[...] + (1.0 - DECAY_RATE) * collect(ff_buf, ff_sems) / d_full
    ff_res[...] = ff_new
    put(ff_res, ff_out, blocks)
    inv = 1.0 / ff_new

    q_part = [jnp.zeros((8, LANES), jnp.float32)] * lane_blocks
    for k in range(blocks):
        rows = pl.ds(k * LANES, LANES)
        u = jnp.broadcast_to(inv[k:k + 1], (LANES, LANES)).T
        for j in range(lane_blocks):
            v = g_ref[rows, pl.ds(j * LANES, LANES)]
            q_part[j] = q_part[j] + jnp.sum((v * v * u).reshape(LANES // 8, 8, LANES), axis=0)
    for j in range(lane_blocks):
        q_buf[pl.ds(j, 1), :] = jnp.sum(q_part[j], axis=0, keepdims=True)

    d_new = DECAY_RATE * d_prev[...] + (1.0 - DECAY_RATE) * collect(dcol_buf, dcol_sems) / ff_full
    d_res[...] = d_new
    put(d_res, d_out, blocks + 1)

    def whole(v):
        return jnp.sum(jnp.sum(v, axis=0, keepdims=True), axis=1, keepdims=True)

    here = col * n_dp + dp
    lane = lax.broadcasted_iota(jnp.int32, (1, LANES), 1)
    xy_buf[here] = jnp.where(lane < LANES // 2, whole(q_buf[...] / d_new), whole(ff_new))
    spread(xy_buf, here, xy_sems, [{**c, **d} for c in cols_far + [{"col": col}] for d in dps_far + [{"dp": dp}]][:-1])
    total = collect(xy_buf, xy_sems)
    ff_mean = total[:, LANES - 1:] / ff_full
    t_buf[row] = total
    inv_d = lax.rsqrt(d_new)
    inv_f = lax.rsqrt(ff_new)

    def scale():
        for k in range(blocks):
            rows = pl.ds(k * LANES, LANES)
            u = jnp.broadcast_to(inv_f[k:k + 1], (LANES, LANES)).T
            for j in range(lane_blocks):
                cols = pl.ds(j * LANES, LANES)
                g_ref[rows, cols] = g_ref[rows, cols] * u * inv_d[j:j + 1]
            put(g_ref.at[rows], g_out.at[rows], k)

    spread(t_buf, row, t_sems, rows_far)
    scale()
    for c in sends:
        c.wait_send()
    for buf, sems in ((ff_buf, ff_sems), (d_buf, d_sems), (dcol_buf, dcol_sems), (xy_buf, xy_sems)):
        slots(buf, sems).wait_send()
    for c in outs:
        c.wait()
    t_total = collect(t_buf, t_sems)
    square_mean = t_total[:, :1] * ff_mean / (d_full * ff_full)
    factor = jnp.sqrt(ff_mean) / jnp.maximum(1.0, jnp.sqrt(square_mean))
    fac_res[...] = jnp.broadcast_to(factor, fac_res.shape)
    put(fac_res, fac_out, blocks + 2)
    slots(t_buf, t_sems).wait_send()
    outs[-1].wait()


def write_kernel(g, fac, w, ff_in, d_in, upd, new, ff_out, d_out, g_buf, fac_buf, w_buf, upd_buf, new_buf, in_sem, out_sem):
    n = g.shape[0] // LANES
    chunk = [pl.ds(k * LANES, LANES) for k in range(n)]
    loads = [pltpu.make_async_copy(fac, fac_buf, in_sem.at[0, n])]
    for k, rows in enumerate(chunk):
        loads.append(pltpu.make_async_copy(g.at[rows], g_buf.at[rows], in_sem.at[0, k]))
        loads.append(pltpu.make_async_copy(w.at[rows], w_buf.at[rows], in_sem.at[1, k]))
    for c in loads:
        c.start()
    loads[0].wait()
    factor = fac_buf[0:1, 0:1]
    copies = [pltpu.make_async_copy(ff_in, ff_out, out_sem.at[0, n]), pltpu.make_async_copy(d_in, d_out, out_sem.at[1, n])]
    for c in copies:
        c.start()
    for k, rows in enumerate(chunk):
        loads[2 * k + 1].wait()
        loads[2 * k + 2].wait()
        clipped = g_buf[rows, :] * factor
        upd_buf[rows, :] = clipped.astype(jnp.bfloat16)
        new_buf[rows, :] = (w_buf[rows, :].astype(jnp.float32) - LEARNING_RATE * clipped).astype(jnp.bfloat16)
        for i, (src, dst) in enumerate(((upd_buf, upd), (new_buf, new))):
            c = pltpu.make_async_copy(src.at[rows], dst.at[rows], out_sem.at[i, k])
            c.start()
            copies.append(c)
    for c in copies:
        c.wait()


def solution(mesh):
    sizes = n_dp, n_row, n_col = tuple(mesh.shape[a] for a in ("dp", "row", "col"))

    def body(inputs, out_grad, weight, ff_old, d_old):
        tok, width = inputs.shape
        units = weight.shape[0]
        hbm = pl.BlockSpec(memory_space=pltpu.HBM)
        f32, bf16 = jnp.float32, jnp.bfloat16
        fr, dr = units // LANES, width // LANES
        dma = pltpu.SemaphoreType.DMA
        shape, vmem = jax.ShapeDtypeStruct, pltpu.VMEM
        g, ff_new, d_new, fac = pl.pallas_call(
            functools.partial(gather_kernel, sizes, float(width * n_row), float(units * n_dp * n_col)),
            out_shape=(shape((units, width), f32), shape((fr, LANES), f32), shape((dr, LANES), f32), shape((8, LANES), f32)),
            in_specs=[hbm] * 4,
            out_specs=(hbm,) * 4,
            scratch_shapes=[
                vmem((units, width), f32),
                vmem((PIECES, n_dp, tok, units // PIECES), bf16),
                vmem((n_dp, tok, width), bf16),
                vmem((fr, LANES), f32),
                vmem((dr, LANES), f32),
                vmem((fr, LANES), f32),
                vmem((dr, LANES), f32),
                vmem((8, LANES), f32),
                vmem((n_row, fr, LANES), f32),
                vmem((n_dp, dr, LANES), f32),
                vmem((n_col, dr, LANES), f32),
                vmem((dr, LANES), f32),
                vmem((n_dp * n_col, 1, LANES), f32),
                vmem((n_row, 1, LANES), f32),
                dma((6,)), dma((PIECES, n_dp)), dma((2, n_dp)),
                dma((3,)), dma((5, n_dp)), dma((4, n_dp)),
                dma((5, n_dp)), dma((PIECES + 1,)), dma((5, n_dp)), dma((6,)), dma((fr + 3,)),
                dma((2,)), dma((2,)), dma((2,)), dma((2,)), dma((2,)),
                pltpu.SemaphoreType.REGULAR((2,)),
            ],
            compiler_params=pltpu.CompilerParams(collective_id=0, has_side_effects=True, vmem_limit_bytes=56 * 2**20),
            name="gather_product_stats",
        )(inputs, out_grad, ff_old.reshape(fr, LANES), d_old.reshape(dr, LANES))
        upd, new, ff_res, d_res = pl.pallas_call(
            write_kernel,
            out_shape=(shape((units, width), bf16), shape((units, width), bf16), shape((fr, LANES), f32), shape((dr, LANES), f32)),
            in_specs=[hbm] * 5,
            out_specs=(hbm,) * 4,
            scratch_shapes=[
                vmem((units, width), f32),
                vmem((8, LANES), f32),
                vmem((units, width), bf16),
                vmem((units, width), bf16),
                vmem((units, width), bf16),
                dma((2, fr + 1)),
                dma((2, fr + 1)),
            ],
            compiler_params=pltpu.CompilerParams(vmem_limit_bytes=56 * 2**20),
            name="write_results",
        )(g, fac, weight, ff_new, d_new)
        return upd, new, ff_res.reshape(units), d_res.reshape(width)

    return jax.shard_map(
        body,
        mesh=mesh,
        in_specs=(
            P("dp", "row"),
            P("dp", "col"),
            P(("col", "dp"), "row"),
            P(("col", "dp")),
            P("row"),
        ),
        out_specs=(P(("col", "dp"), "row"), P(("col", "dp"), "row"), P(("col", "dp")), P("row")),
        check_vma=False,
    )
```

```python
import functools

import jax
import jax.numpy as jnp
from jax import lax
from jax.experimental import pallas as pl
from jax.experimental.pallas import tpu as pltpu
from jax.sharding import PartitionSpec as P

D = 9216
FF = 49152

DECAY_RATE = 1.0 - 10.0 ** (-0.8)
SQUARE_EPS = 1e-30
LEARNING_RATE = 0.02

MESH = pl.DeviceIdType.MESH
LANES = 128
CHUNK = 256
PIECES = 3
QUARTERS = 4


def gather_kernel(sizes, d_full, ff_full, inp, og, ff_old, d_old, g_out, ff_out, d_out, fac_out,
                  g_ref, a_buf, b_buf, ff_prev, d_prev, ff_res, d_res, fac_res, ff_buf, d_buf, dcol_buf, q_buf, xy_buf, t_buf,
                  a_send, a_recv, z_send, b_send, b_recv, y_send, c_send, sib_send, c_recv, loc, out_sem,
                  ff_sems, d_sems, dcol_sems, xy_sems, t_sems, heard):
    n_dp, n_row, n_col = sizes
    n_x = n_dp // 2
    dp, row, col = (lax.axis_index(a) for a in ("dp", "row", "col"))
    x = dp // 2
    core = dp - 2 * x
    sib = 2 * x + 1 - core
    m = lax.rem(row, PIECES)
    q = lax.rem(col, QUARTERS)
    tok, width = inp.shape
    units = g_ref.shape[0]
    piece = units // PIECES
    quarter = tok // QUARTERS
    half = quarter // 2
    blocks = units // LANES
    lane_blocks = width // LANES

    barrier = pltpu.get_barrier_semaphore()
    def others(axis, n, me):
        order = sorted(range(1, n), key=lambda t: -min(t, n - t))
        return [{axis: lax.rem(me + t, n)} for t in order]

    rows_far, cols_far, dps_far = others("row", n_row, row), others("col", n_col, col), others("dp", n_dp, dp)
    greeted = rows_far[-2:] + cols_far[-4:] + dps_far
    for there in greeted:
        pl.semaphore_signal(barrier, inc=1, device_id=there, device_id_type=MESH)

    def og_piece(to, p):
        return og.at[:, pl.ds(pl.multiple_of(to * units + p * piece, LANES), piece)]

    def rows_of(start, size):
        return pl.ds(pl.multiple_of(start, 16), size)

    own = [pltpu.make_async_copy(og_piece(dp, p), a_buf.at[p, dp], loc.at[p]) for p in range(PIECES)]
    own.append(pltpu.make_async_copy(inp, b_buf.at[dp], loc.at[3]))
    own.append(pltpu.make_async_copy(ff_old, ff_prev, loc.at[4]))
    own.append(pltpu.make_async_copy(d_old, d_prev, loc.at[5]))
    for c in own:
        c.start()

    def far(dx, flip):
        there = lax.rem(x + dx + n_x, n_x)
        return 2 * there + (1 - core if flip else core)

    def send_a(k, dx, flip):
        to = far(dx, flip)
        return pltpu.make_async_remote_copy(og_piece(to, m), a_buf.at[m, dp], a_send.at[k], a_recv.at[0, dp],
                                            device_id={"dp": to}, device_id_type=MESH)

    def send_sib_a(j):
        p = lax.rem(m + j, PIECES)
        return pltpu.make_async_remote_copy(og_piece(sib, p), a_buf.at[p, dp], sib_send.at[j], a_recv.at[j, dp],
                                            device_id={"dp": sib}, device_id_type=MESH)

    def send_b(k, dx):
        part = rows_of(q * quarter, quarter)
        return pltpu.make_async_remote_copy(inp.at[part], b_buf.at[dp, part], b_send.at[k], b_recv.at[0, dp],
                                            device_id={"dp": far(dx, False)}, device_id_type=MESH)

    def pass_z(src, j):
        to = lax.rem(row + (n_row - 1 if j == 1 else 1), n_row)
        return pltpu.make_async_remote_copy(a_buf.at[m, src], a_buf.at[m, src], z_send.at[j - 1, src], a_recv.at[j, src],
                                            device_id={"row": to}, device_id_type=MESH)

    def pass_y(src, j):
        step = (1, -1, 2, -2)[j - 1]
        start, size = q * quarter, quarter
        if j >= 3:
            start, size = start + (j - 3) * half, half
        part = rows_of(start, size)
        return pltpu.make_async_remote_copy(b_buf.at[src, part], b_buf.at[src, part], y_send.at[j - 1, src], b_recv.at[j, src],
                                            device_id={"col": lax.rem(col + step + n_col, n_col)}, device_id_type=MESH)

    def part_of(j):
        shift = (0, -1, 1, -2, 2)[j]
        start, size = lax.rem(q + shift + QUARTERS, QUARTERS) * quarter, quarter
        if j >= 3:
            start, size = start + (j - 3) * half, half
        return rows_of(start, size)

    def share(src, j):
        part = part_of(j)
        return pltpu.make_async_remote_copy(b_buf.at[src, part], b_buf.at[src, part], c_send.at[j, src], c_recv.at[j, src],
                                            device_id={"dp": sib}, device_id_type=MESH)

    def got_a(j, src):
        p = lax.rem(m + j, PIECES)
        pltpu.make_async_remote_copy(a_buf.at[p, src], a_buf.at[p, src], a_send.at[0], a_recv.at[j, src],
                                     device_id={"dp": sib}, device_id_type=MESH).wait_recv()

    def got_b(j, src, recv):
        part = part_of(j)
        pltpu.make_async_remote_copy(b_buf.at[src, part], b_buf.at[src, part], b_send.at[0], recv.at[j, src],
                                     device_id={"dp": sib}, device_id_type=MESH).wait_recv()

    near = ((1, False), (-1, False), (1, True), (-1, True))
    away = ((2, False), (2, True))
    steps = (1, -1, 2)
    order = ("n0", "n1", "b0", "b1", "n2", "n3", "w0", "b2", "w1")
    moves = {}
    for k, t in enumerate(near):
        moves["n" + str(k)] = send_a(k, *t)
    for k, t in enumerate(away):
        moves["w" + str(k)] = send_a(len(near) + k, *t)
    for k, dx in enumerate(steps):
        moves["b" + str(k)] = send_b(k, dx)
    sends = [moves[k] for k in order]
    sends += [send_sib_a(j) for j in range(PIECES)]

    pl.semaphore_wait(barrier, len(greeted))

    def hail():
        for i, there in enumerate(rows_far[-2:]):
            pl.semaphore_signal(heard.at[i], inc=1, device_id=there, device_id_type=MESH)

    def answered():
        for i in range(2):
            pl.semaphore_wait(heard.at[i], 1)

    hail()
    for c in sends:
        c.start()

    def go(c):
        c.start()
        sends.append(c)

    own[3].wait()
    go(pltpu.make_async_remote_copy(b_buf.at[dp], b_buf.at[dp], sib_send.at[PIECES], c_recv.at[0, dp],
                                    device_id={"dp": sib}, device_id_type=MESH))

    def product(j, chip, first=False):
        p = lax.rem(m + j, PIECES)
        out = g_ref.at[pl.ds(pl.multiple_of(p * piece, LANES), piece)]
        pair = pl.ds(2 * chip, 2)
        value = lax.dot_general(a_buf[p, pair].reshape(2 * tok, piece), b_buf[pair].reshape(2 * tok, width),
                                (((0,), (0,)), ((), ())), preferred_element_type=jnp.float32)
        out[...] = value if first else out[...] + value

    def relay_a(dx, flip):
        src = far(dx, flip)
        got_a(0, src)
        go(pass_z(src, 1))
        go(pass_z(src, 2))

    def relay_b(dx):
        src = far(dx, False)
        got_b(0, src, b_recv)
        for j in (1, 2, 3, 4):
            go(pass_y(src, j))
        go(share(src, 0))

    def collect_b(dx):
        src = far(dx, False)
        for j in (1, 2, 3, 4):
            got_b(j, src, b_recv)
            go(share(src, j))

    def take(dx, j):
        got_a(j, far(dx, False)) if j else None
        got_a(j, far(dx, True)) if j else None
        product(j, lax.rem(x + dx + n_x, n_x))

    def relay(name):
        k = int(name[1])
        if name[0] == "b":
            relay_b(steps[k])
        else:
            relay_a(*(near if name[0] == "n" else away)[k])

    for k, name in enumerate(order[:-2]):
        relay(name)
        if k in (1, 4, 6):
            answered()
            hail()
    for c in own[:3]:
        c.wait()
    pltpu.make_async_remote_copy(b_buf.at[sib], b_buf.at[sib], b_send.at[0], c_recv.at[0, sib],
                                 device_id={"dp": sib}, device_id_type=MESH).wait_recv()
    for j in range(PIECES):
        got_a(j, sib)
        product(j, x, first=True)
    own[4].wait()
    own[5].wait()

    d_part = [jnp.zeros((8, LANES), jnp.float32)] * lane_blocks

    def squares(j):
        p = lax.rem(m + j, PIECES)
        for i in range(piece // LANES):
            rows = pl.ds(pl.multiple_of(p * piece, LANES) + i * LANES, LANES)
            part = None
            for k in range(lane_blocks):
                v = g_ref[rows, pl.ds(k * LANES, LANES)]
                sq = v * v + SQUARE_EPS
                part = sq if part is None else part + sq
                d_part[k] = d_part[k] + jnp.sum(sq.reshape(LANES // 8, 8, LANES), axis=0)
            ff_buf[row, pl.ds(p * (piece // LANES) + i, 1), :] = jnp.sum(part.T, axis=0, keepdims=True)

    def takes(dx):
        for j in range(5):
            got_b(j, far(dx, True), c_recv)
        for j in range(PIECES):
            take(dx, j)
            if dx == steps[-1]:
                squares(j)

    collect_b(steps[0])
    relay(order[-2])
    collect_b(steps[1])
    answered()
    hail()
    takes(steps[0])
    relay(order[-1])
    takes(steps[1])
    collect_b(steps[2])
    answered()
    takes(steps[2])
    for k in range(lane_blocks):
        d_buf[dp, pl.ds(k, 1), :] = jnp.sum(d_part[k], axis=0, keepdims=True)

    def spread(buf, me, sems, targets):
        for there in targets:
            pltpu.make_async_remote_copy(buf.at[me], buf.at[me], sems.at[0], sems.at[1],
                                         device_id=there, device_id_type=MESH).start()

    def slots(buf, sems):
        rest = buf.at[pl.ds(0, buf.shape[0] - 1)]
        return pltpu.make_async_remote_copy(rest, rest, sems.at[0], sems.at[1], device_id={"dp": sib}, device_id_type=MESH)

    def collect(buf, sems):
        slots(buf, sems).wait_recv()
        terms = [buf[k] for k in range(buf.shape[0])]
        while len(terms) > 1:
            terms = [sum(terms[k + 1:k + 2], terms[k]) for k in range(0, len(terms), 2)]
        return terms[0]

    outs = []

    def put(src, dst, k):
        c = pltpu.make_async_copy(src, dst, out_sem.at[k])
        c.start()
        outs.append(c)

    spread(d_buf, dp, d_sems, dps_far)
    spread(ff_buf, row, ff_sems, rows_far)
    dcol_buf[col] = collect(d_buf, d_sems)
    spread(dcol_buf, col, dcol_sems, cols_far)
    ff_new = DECAY_RATE * ff_prev[...] + (1.0 - DECAY_RATE) * collect(ff_buf, ff_sems) / d_full
    ff_res[...] = ff_new
    put(ff_res, ff_out, blocks)
    inv = 1.0 / ff_new

    q_part = [jnp.zeros((8, LANES), jnp.float32)] * lane_blocks
    for k in range(blocks):
        rows = pl.ds(k * LANES, LANES)
        u = jnp.broadcast_to(inv[k:k + 1], (LANES, LANES)).T
        for j in range(lane_blocks):
            v = g_ref[rows, pl.ds(j * LANES, LANES)]
            q_part[j] = q_part[j] + jnp.sum((v * v * u).reshape(LANES // 8, 8, LANES), axis=0)
    for j in range(lane_blocks):
        q_buf[pl.ds(j, 1), :] = jnp.sum(q_part[j], axis=0, keepdims=True)

    d_new = DECAY_RATE * d_prev[...] + (1.0 - DECAY_RATE) * collect(dcol_buf, dcol_sems) / ff_full
    d_res[...] = d_new
    put(d_res, d_out, blocks + 1)

    def whole(v):
        return jnp.sum(jnp.sum(v, axis=0, keepdims=True), axis=1, keepdims=True)

    here = col * n_dp + dp
    lane = lax.broadcasted_iota(jnp.int32, (1, LANES), 1)
    xy_buf[here] = jnp.where(lane < LANES // 2, whole(q_buf[...] / d_new), whole(ff_new))
    spread(xy_buf, here, xy_sems, [{**c, **d} for c in cols_far + [{"col": col}] for d in dps_far + [{"dp": dp}]][:-1])
    total = collect(xy_buf, xy_sems)
    ff_mean = total[:, LANES - 1:] / ff_full
    t_buf[row] = total
    inv_d = lax.rsqrt(d_new)
    inv_f = lax.rsqrt(ff_new)

    def scale():
        for k in range(blocks):
            rows = pl.ds(k * LANES, LANES)
            u = jnp.broadcast_to(inv_f[k:k + 1], (LANES, LANES)).T
            for j in range(lane_blocks):
                cols = pl.ds(j * LANES, LANES)
                g_ref[rows, cols] = g_ref[rows, cols] * u * inv_d[j:j + 1]
            put(g_ref.at[rows], g_out.at[rows], k)

    spread(t_buf, row, t_sems, rows_far)
    scale()
    for c in sends:
        c.wait_send()
    for buf, sems in ((ff_buf, ff_sems), (d_buf, d_sems), (dcol_buf, dcol_sems), (xy_buf, xy_sems)):
        slots(buf, sems).wait_send()
    for c in outs:
        c.wait()
    t_total = collect(t_buf, t_sems)
    square_mean = t_total[:, :1] * ff_mean / (d_full * ff_full)
    factor = jnp.sqrt(ff_mean) / jnp.maximum(1.0, jnp.sqrt(square_mean))
    fac_res[...] = jnp.broadcast_to(factor, fac_res.shape)
    put(fac_res, fac_out, blocks + 2)
    slots(t_buf, t_sems).wait_send()
    outs[-1].wait()


def write_kernel(g, fac, w, ff_in, d_in, upd, new, ff_out, d_out, g_buf, fac_buf, w_buf, upd_buf, new_buf, in_sem, out_sem):
    n = g.shape[0] // CHUNK
    chunk = [pl.ds(k * CHUNK, CHUNK) for k in range(n)]
    loads = [pltpu.make_async_copy(fac, fac_buf, in_sem.at[0, n])]
    for k, rows in enumerate(chunk):
        loads.append(pltpu.make_async_copy(g.at[rows], g_buf.at[rows], in_sem.at[0, k]))
        loads.append(pltpu.make_async_copy(w.at[rows], w_buf.at[rows], in_sem.at[1, k]))
    for c in loads:
        c.start()
    copies = [pltpu.make_async_copy(ff_in, ff_out, out_sem.at[0, n]), pltpu.make_async_copy(d_in, d_out, out_sem.at[1, n])]
    for c in copies:
        c.start()
    loads[0].wait()
    factor = fac_buf[0:1, 0:1]
    for k, rows in enumerate(chunk):
        loads[2 * k + 1].wait()
        loads[2 * k + 2].wait()
        clipped = g_buf[rows, :] * factor
        upd_buf[rows, :] = clipped.astype(jnp.bfloat16)
        new_buf[rows, :] = (w_buf[rows, :].astype(jnp.float32) - LEARNING_RATE * clipped).astype(jnp.bfloat16)
        for i, (src, dst) in enumerate(((upd_buf, upd), (new_buf, new))):
            c = pltpu.make_async_copy(src.at[rows], dst.at[rows], out_sem.at[i, k])
            c.start()
            copies.append(c)
    for c in copies:
        c.wait()


def solution(mesh):
    sizes = n_dp, n_row, n_col = tuple(mesh.shape[a] for a in ("dp", "row", "col"))

    def body(inputs, out_grad, weight, ff_old, d_old):
        tok, width = inputs.shape
        units = weight.shape[0]
        hbm = pl.BlockSpec(memory_space=pltpu.HBM)
        f32, bf16 = jnp.float32, jnp.bfloat16
        fr, dr = units // LANES, width // LANES
        dma = pltpu.SemaphoreType.DMA
        shape, vmem = jax.ShapeDtypeStruct, pltpu.VMEM
        g, ff_new, d_new, fac = pl.pallas_call(
            functools.partial(gather_kernel, sizes, float(width * n_row), float(units * n_dp * n_col)),
            out_shape=(shape((units, width), f32), shape((fr, LANES), f32), shape((dr, LANES), f32), shape((8, LANES), f32)),
            in_specs=[hbm] * 4,
            out_specs=(hbm,) * 4,
            scratch_shapes=[
                vmem((units, width), f32),
                vmem((PIECES, n_dp, tok, units // PIECES), bf16),
                vmem((n_dp, tok, width), bf16),
                vmem((fr, LANES), f32),
                vmem((dr, LANES), f32),
                vmem((fr, LANES), f32),
                vmem((dr, LANES), f32),
                vmem((8, LANES), f32),
                vmem((n_row, fr, LANES), f32),
                vmem((n_dp, dr, LANES), f32),
                vmem((n_col, dr, LANES), f32),
                vmem((dr, LANES), f32),
                vmem((n_dp * n_col, 1, LANES), f32),
                vmem((n_row, 1, LANES), f32),
                dma((6,)), dma((PIECES, n_dp)), dma((2, n_dp)),
                dma((3,)), dma((5, n_dp)), dma((4, n_dp)),
                dma((5, n_dp)), dma((PIECES + 1,)), dma((5, n_dp)), dma((6,)), dma((fr + 3,)),
                dma((2,)), dma((2,)), dma((2,)), dma((2,)), dma((2,)),
                pltpu.SemaphoreType.REGULAR((2,)),
            ],
            compiler_params=pltpu.CompilerParams(collective_id=0, has_side_effects=True, vmem_limit_bytes=56 * 2**20),
            name="gather_product_stats",
        )(inputs, out_grad, ff_old.reshape(fr, LANES), d_old.reshape(dr, LANES))
        upd, new, ff_res, d_res = pl.pallas_call(
            write_kernel,
            out_shape=(shape((units, width), bf16), shape((units, width), bf16), shape((fr, LANES), f32), shape((dr, LANES), f32)),
            in_specs=[hbm] * 5,
            out_specs=(hbm,) * 4,
            scratch_shapes=[
                vmem((units, width), f32),
                vmem((8, LANES), f32),
                vmem((units, width), bf16),
                vmem((units, width), bf16),
                vmem((units, width), bf16),
                dma((2, units // CHUNK + 1)),
                dma((2, units // CHUNK + 1)),
            ],
            compiler_params=pltpu.CompilerParams(vmem_limit_bytes=56 * 2**20),
            name="write_results",
        )(g, fac, weight, ff_new, d_new)
        return upd, new, ff_res.reshape(units), d_res.reshape(width)

    return jax.shard_map(
        body,
        mesh=mesh,
        in_specs=(
            P("dp", "row"),
            P("dp", "col"),
            P(("col", "dp"), "row"),
            P(("col", "dp")),
            P("row"),
        ),
        out_specs=(P(("col", "dp"), "row"), P(("col", "dp"), "row"), P(("col", "dp")), P("row")),
        check_vma=False,
    )
```
